32 devices in a mesh: amp: 8 (over z, x), int: 4 (over y, core).
Axes of the slice: x: 2, y: 2, z: 4, core: 2. Of those that a mesh axis runs over, the one named last changes fastest.
Arguments:
- t2_stored: float32 [1024, 4096], P('amp', 'int'), may hold values from -6 to 6
- integrals: float32 [4096, 4096], P('amp', 'int'), may hold values from -0.09375 to 0.09375
- driver: float32 [1024, 4096], P('amp', 'int'), may hold values from -6 to 6
- eps_occ: float32 [120], replicated, may hold values from -2 to -0.3
- eps_vir: float32 [600], replicated, may hold values from 0.1 to 3
- blk_len: int32 [32], replicated, may hold values from 32 to 128, as said below
- t2_order: int32 [32], replicated, may hold values from 0 to 31, as said below
- int_order: int32 [32], replicated, may hold values from 0 to 31, as said below
Outputs:
- update: float32 [1024, 4096], P('amp', 'int')
The draws below stay inside these ranges and needn't reach their ends.
Inputs may be any that keep to these rules, and one draw needn't show every extreme that they name: `blk_len`: live slots of a block come first; some block is full and some has 32 live slots. `int_order`: a permutation of the blocks; the integrals' row blocks on one amp index are int_order's blocks of that index. `t2_order`: a permutation of the blocks; the stored column blocks on each int index hold exactly one of the blocks that int_order places on each amp index.
All inputs are finite; a program needn't handle non-finite values.
Results may differ from the reference program's by a relative error of at most 0.00005.
Values sent between devices are 32-bit elements; how exact they have to be, the bound alone decides.
A program may use at most 128 MiB of HBM per device.

```python
import jax
import jax.numpy as jnp
from jax import lax

NO = 120
NV = 600
TILE = 128
NBLK = 32
PAIRS = 4096
OPAIRS = 1024
N_AMP = 8


def draw_blk_len(key, part):
    lengths = jax.random.randint(jax.random.fold_in(key, 1), (NBLK,), TILE // 4, TILE + 1)
    spots = jax.random.permutation(jax.random.fold_in(key, 2), NBLK)
    lengths = lengths.at[spots[0]].set(TILE).at[spots[1]].set(TILE // 4)
    return lengths.astype(jnp.int32)


def shuffle_row(row_key, values):
    return jax.random.permutation(row_key, values)


def block_orders(key):
    base = jax.random.fold_in(key, 11)
    integral_order = jax.random.permutation(jax.random.fold_in(base, 1), NBLK).astype(jnp.int32)
    owned_rows = integral_order.reshape(N_AMP, NBLK // N_AMP)
    first_keys = jax.random.split(jax.random.fold_in(base, 2), N_AMP)
    shuffled = jax.vmap(shuffle_row)(first_keys, owned_rows)
    per_slice = shuffled.T
    second_keys = jax.random.split(jax.random.fold_in(base, 3), NBLK // N_AMP)
    per_slice = jax.vmap(shuffle_row)(second_keys, per_slice)
    return (per_slice.reshape(NBLK).astype(jnp.int32), integral_order)


def draw_t2_order(key, part):
    return block_orders(key)[0]


def draw_int_order(key, part):
    return block_orders(key)[1]


def steps_of(own_key, dims, cuts, least, top_value):
    gain = 1.0
    for position, parts in cuts:
        draws = jax.random.uniform(jax.random.fold_in(jax.random.fold_in(own_key, 6), position), (parts,), jnp.float32, least / len(cuts), top_value / len(cuts))
        gain = gain * jnp.repeat(jnp.exp(draws), dims[position] // parts).reshape((-1,) + (1,) * (len(dims) - 1 - position))
    return gain


def normal_values(own_key, shape, scale, bound, cuts=(), kind=jnp.bfloat16):
    array = jax.random.normal(own_key, shape, jnp.float32) * scale
    if len(cuts) > 0:
        array = steps_of(own_key, shape, cuts, -0.22, 0.18) * array
    return jnp.clip(array, min=-bound, max=bound).astype(kind)


def setup_inputs(seed: int = 0) -> dict:
    seeds = jax.random.split(jax.random.key(seed), 9)
    return {
        "t2_stored": normal_values(seeds[0], (OPAIRS, PAIRS), 1.0, 6.0, ((0, 8), (1, 4)), jnp.float32),
        "integrals": normal_values(seeds[1], (PAIRS, PAIRS), PAIRS ** -0.5, 0.09375, ((0, 8), (1, 4)), jnp.float32),
        "driver": normal_values(seeds[2], (OPAIRS, PAIRS), 1.0, 6.0, ((0, 8), (1, 4)), jnp.float32),
        "eps_occ": jnp.clip(jax.random.uniform(seeds[3], (NO,), jnp.float32, -2.0, -0.3), -2.0, -0.3),
        "eps_vir": jnp.clip(jax.random.uniform(seeds[4], (NV,), jnp.float32, 0.1, 3.0), 0.1, 3.0),
        "blk_len": draw_blk_len(jax.random.fold_in(seeds[8], 71), 0),
        "t2_order": draw_t2_order(jax.random.fold_in(seeds[8], 71), 0),
        "int_order": draw_int_order(jax.random.fold_in(seeds[8], 71), 0),
    }


def reference(t2_stored, integrals, driver, eps_occ, eps_vir, blk_len, t2_order, int_order):
    slot_index = jnp.arange(TILE, dtype=jnp.int32)
    live_mask = (slot_index[None, :] < blk_len[:, None]).astype(jnp.float32)
    counter = jnp.arange(NBLK, dtype=jnp.int32)
    inverse_t2 = jnp.zeros((NBLK,), jnp.int32).at[t2_order].set(counter)
    source_block = inverse_t2[int_order]
    blocks = t2_stored.reshape(OPAIRS, NBLK, TILE)
    picked = blocks[:, source_block, :] * live_mask[int_order][None, :, :]
    amplitudes = picked.reshape(OPAIRS, PAIRS)
    ladder = jnp.dot(amplitudes, integrals, precision=lax.Precision.HIGHEST, preferred_element_type=jnp.float32)
    residual = driver + ladder
    row_ids = jnp.arange(OPAIRS, dtype=jnp.int32)
    col_ids = jnp.arange(PAIRS, dtype=jnp.int32)
    occ_first = row_ids // NO
    occ_second = row_ids % NO
    vir_first = col_ids % NV
    vir_second = (3 * col_ids + col_ids // NV) % NV
    denominators = eps_vir[vir_first][None, :] + eps_vir[vir_second][None, :] - eps_occ[occ_first][:, None] - eps_occ[occ_second][:, None]
    live_cols = live_mask.reshape(PAIRS)
    return residual * live_cols[None, :] / denominators
```

```python
import functools

import jax
import jax.numpy as jnp
from jax import lax
from jax.experimental import pallas as pl
from jax.experimental.pallas import tpu as pltpu
from jax.sharding import PartitionSpec as P

NO = 120
NV = 600
TILE = 128
WIDTH = 128
MESH = pl.DeviceIdType.MESH


def split_index(ids, size):
    quotient = ((ids.astype(jnp.float32) + 0.5) * (1.0 / size)).astype(jnp.int32)
    return quotient, ids - quotient * size


def halves(values):
    high = values.astype(jnp.bfloat16)
    return high, (values - high.astype(jnp.float32)).astype(jnp.bfloat16)


def kernel(
    n_amp, n_int,
    t2_order, int_order, blk_len, t2, own_b, driver, eps_occ, eps_vir, out,
    unit, gathered, a_high, a_low, other_b, partial, arrived, vir_sum,
    b_send, b_recv, u_send, u_recv, y_send, core_send, g_recv, r_send, r_recv,
):
    amp = lax.axis_index("amp")
    q = lax.axis_index("int")
    groups = n_amp // 2
    ys = n_int // 2
    g, h = amp // 2, amp % 2
    y, core = q // 2, q % 2
    rows = t2.shape[0]
    slots = t2.shape[1] // TILE
    owned = own_b.shape[0] // TILE
    chunks = own_b.shape[1] // WIDTH
    partner = (g * 2 + 1 - h, q)
    sibling = (amp, y * 2 + 1 - core)

    def member(group):
        return (group * 2 + h, q)

    peers = [partner, sibling]
    peers += [member((g + k) % groups) for k in range(1, groups)]
    peers += [(amp, (y + k) % ys * 2 + core) for k in range(1, ys)]
    barrier = pltpu.get_barrier_semaphore()
    for peer in peers:
        pl.semaphore_signal(barrier, inc=1, device_id=peer, device_id_type=MESH)
    pl.semaphore_wait(barrier, len(peers))

    def remote(src, dst, send, recv, peer):
        return pltpu.make_async_remote_copy(
            src_ref=src, dst_ref=dst, send_sem=send, recv_sem=recv, device_id=peer, device_id_type=MESH
        )

    def b_copy(c):
        cols = pl.ds(pl.multiple_of(c * WIDTH, WIDTH), WIDTH)
        return remote(own_b.at[:, cols], other_b.at[c], b_send.at[c], b_recv.at[c], partner)

    @pl.loop(0, chunks)
    def _(c):
        b_copy(c).start()

    lane = lax.broadcasted_iota(jnp.int32, (rows, TILE), 1)

    def u_copy(group):
        return remote(unit.at[group], gathered.at[q, g], u_send.at[group], u_recv.at[g], member(group))

    def u_arrival(group):
        return remote(unit.at[group], gathered.at[q, group], u_send.at[group], u_recv.at[group], member(group))

    stored = [t2_order[q * slots + k] for k in range(slots)]
    lengths = []
    for k in range(slots):
        length = jnp.int32(0)
        for b in range(n_amp * owned):
            length += (stored[k] == b).astype(jnp.int32) * blk_len[b]
        lengths.append(length)

    def build(group):
        for side in range(2):
            p = group * 2 + (h if side == 0 else 1 - h)
            wanted = [int_order[p * owned + j] for j in range(owned)]
            total = jnp.zeros((rows, TILE), jnp.float32)
            for k in range(slots):
                held = jnp.int32(0)
                for block in wanted:
                    held += (stored[k] == block).astype(jnp.int32)
                total = jnp.where(lane < held * lengths[k], t2[:, k * TILE:(k + 1) * TILE], total)
            unit[group, :, side * TILE:(side + 1) * TILE] = total

    for k in range(1, groups):
        group = (g + k) % groups
        build(group)
        u_copy(group).start()
    build(g)
    gathered[q, g] = unit[g]

    def y_copy(k, group):
        return remote(
            gathered.at[q, group], gathered.at[q, group], y_send.at[k, group], g_recv.at[q, group],
            (amp, (y + k) % ys * 2 + core),
        )

    def core_copy(row, group):
        return remote(
            gathered.at[row, group], gathered.at[row, group], core_send.at[row, group], g_recv.at[row, group], sibling
        )

    def arrival(row, group):
        return remote(
            gathered.at[row, group], gathered.at[row, group], core_send.at[row, group], g_recv.at[row, group], sibling
        )

    for k in range(groups):
        group = (g + k) % groups
        if k > 0:
            u_arrival(group).wait_recv()
        for m in range(1, ys):
            y_copy(m, group).start()
        core_copy(q, group).start()


    row_ids = amp * rows + lax.broadcasted_iota(jnp.int32, (rows, NO), 0)
    place = lax.broadcasted_iota(jnp.int32, (rows, NO), 1)
    first, second = split_index(row_ids, NO)
    occ = jnp.broadcast_to(eps_occ[...], (rows, NO))
    occ_first = jnp.sum(jnp.where(place == first, occ, 0.0), axis=1, keepdims=True)
    occ_second = jnp.sum(jnp.where(place == second, occ, 0.0), axis=1, keepdims=True)

    for k in range(groups):
        group = (g + k) % groups
        for m in range(1, ys):
            row = (y + m) % ys * 2 + core
            arrival(row, group).wait_recv()
            core_copy(row, group).start()
    for k in range(groups):
        group = (g + k) % groups
        for m in range(ys):
            arrival((y + m) % ys * 2 + 1 - core, group).wait_recv()
    for side in range(2):
        p = g * 2 + (h if side == 0 else 1 - h)
        for j in range(owned):
            block = int_order[p * owned + j]
            shares = []
            for source in range(n_int):
                share = jnp.int32(0)
                for k in range(slots):
                    share += (t2_order[source * slots + k] == block).astype(jnp.int32)
                shares.append(jnp.full((rows, TILE), share, jnp.int32) > 0)
            for group in range(groups):
                picked = jnp.zeros((rows, TILE), jnp.float32)
                for source in range(n_int):
                    piece = gathered[source, group, :, side * TILE:(side + 1) * TILE]
                    picked = jnp.where(shares[source], piece, picked)
                high, low = halves(picked)
                spot = (pl.ds(group * rows, rows), pl.ds((side * owned + j) * TILE, TILE))
                a_high[spot] = high
                a_low[spot] = low

    def forward_copy(c, d, slot, group):
        return remote(partial.at[c, d], arrived.at[c, slot], r_send.at[c, d], r_recv.at[c, slot], member(group))

    def take_in(c, d, slot):
        remote(
            partial.at[c, d], arrived.at[c, slot], r_send.at[c, d], r_recv.at[c, slot], partner
        ).wait_recv()
        partial[c, d] += arrived[c, slot]

    @pl.loop(0, chunks + groups - 1)
    def _(t):
        @pl.when(t < chunks)
        def _():
            cols = pl.ds(pl.multiple_of(t * WIDTH, WIDTH), WIDTH)
            b_copy(t).wait_recv()
            high, low = halves(jnp.concatenate([own_b[:, cols], other_b[t]], axis=0))
            dot = functools.partial(jnp.dot, preferred_element_type=jnp.float32)
            product = dot(a_low[...], high) + dot(a_high[...], low) + dot(a_high[...], high)
            partial[t] = product.reshape(groups, rows, WIDTH)

            col_ids = q * own_b.shape[1] + t * WIDTH + lax.broadcasted_iota(jnp.int32, (NV, WIDTH), 1)
            spot = lax.broadcasted_iota(jnp.int32, (NV, WIDTH), 0)
            around, first_vir = split_index(col_ids, NV)
            second_vir = split_index(3 * col_ids + around, NV)[1]
            picks = (spot == first_vir).astype(jnp.float32) + (spot == second_vir).astype(jnp.float32)
            vir_sum[t] = jnp.dot(
                jnp.broadcast_to(eps_vir[...], (8, NV)), picks,
                precision=lax.Precision.HIGHEST, preferred_element_type=jnp.float32,
            )

        right = t - g
        left = t - (groups - 1 - g)

        @pl.when((right >= 0) & (right < chunks))
        def _():
            for d in range(groups - 1, 0, -1):
                @pl.when(d > g)
                def _(d=d):
                    @pl.when(g > 0)
                    def _():
                        take_in(right, d, d)
                    forward_copy(right, d, d, g + 1).start()

        @pl.when((left >= 0) & (left < chunks))
        def _():
            for d in range(groups - 1):
                @pl.when(d < g)
                def _(d=d):
                    @pl.when(g < groups - 1)
                    def _():
                        take_in(left, d, d)
                    forward_copy(left, d, jnp.where(d == g - 1, groups, d), g - 1).start()

        done = t - (groups - 1)

        @pl.when(done >= 0)
        def _():
            @pl.when(g > 0)
            def _():
                take_in(done, g, g)

            @pl.when(g < groups - 1)
            def _():
                take_in(done, g, groups)
            cols = pl.ds(pl.multiple_of(done * WIDTH, WIDTH), WIDTH)
            length = blk_len[q * chunks + done]
            live = (lane < length).astype(jnp.float32)
            denominators = vir_sum[done, 0:1, :] - occ_first - occ_second
            out[:, cols] = (driver[:, cols] + partial[done, g]) * live / denominators

    @pl.loop(0, chunks)
    def _(c):
        b_copy(c).wait_send()
        for d in range(groups):
            @pl.when(d != g)
            def _(d=d):
                forward_copy(c, d, d, g).wait_send()
    for k in range(1, groups):
        u_copy((g + k) % groups).wait_send()
    for group in range(groups):
        for m in range(1, ys):
            y_copy(m, group).wait_send()
        for m in range(ys):
            core_copy((y + m) % ys * 2 + core, group).wait_send()


def solution(mesh):
    n_amp, n_int = mesh.shape["amp"], mesh.shape["int"]

    def on_device(t2_stored, integrals, driver, eps_occ, eps_vir, blk_len, t2_order, int_order):
        rows = t2_stored.shape[0]
        depth, cols = integrals.shape
        groups, ys, chunks = n_amp // 2, n_int // 2, cols // WIDTH
        smem = pl.BlockSpec(memory_space=pltpu.SMEM)
        vmem = pl.BlockSpec(memory_space=pltpu.VMEM)
        dma = pltpu.SemaphoreType.DMA
        return pl.pallas_call(
            functools.partial(kernel, n_amp, n_int),
            out_shape=jax.ShapeDtypeStruct((rows, cols), jnp.float32),
            in_specs=[smem] * 3 + [vmem] * 5,
            out_specs=vmem,
            scratch_shapes=[
                pltpu.VMEM((groups, rows, 2 * TILE), jnp.float32),
                pltpu.VMEM((n_int, groups, rows, 2 * TILE), jnp.float32),
                pltpu.VMEM((groups * rows, n_int * 2 * TILE), jnp.bfloat16),
                pltpu.VMEM((groups * rows, n_int * 2 * TILE), jnp.bfloat16),
                pltpu.VMEM((chunks, depth, WIDTH), jnp.float32),
                pltpu.VMEM((chunks, groups, rows, WIDTH), jnp.float32),
                pltpu.VMEM((chunks, groups + 1, rows, WIDTH), jnp.float32),
                pltpu.VMEM((chunks, 8, WIDTH), jnp.float32),
                dma((chunks,)),
                dma((chunks,)),
                dma((groups,)),
                dma((groups,)),
                dma((ys, groups)),
                dma((n_int, groups)),
                dma((n_int, groups)),
                dma((chunks, groups)),
                dma((chunks, groups + 1)),
            ],
            compiler_params=pltpu.CompilerParams(
                collective_id=0, has_side_effects=True, vmem_limit_bytes=60 * 2**20
            ),
            cost_estimate=pl.CostEstimate(flops=6 * rows * groups * depth * 2 * cols, bytes_accessed=2**23, transcendentals=0),
        )(
            t2_order, int_order, blk_len, t2_stored, integrals, driver,
            eps_occ.reshape(1, NO), eps_vir.reshape(1, NV),
        )

    placed = (P("amp", "int"), P("amp", "int"), P("amp", "int"), P(), P(), P(), P(), P())
    return jax.shard_map(on_device, mesh=mesh, in_specs=placed, out_specs=P("amp", "int"), check_vma=False)
```

```python
import functools

import jax
import jax.numpy as jnp
from jax import lax
from jax.experimental import pallas as pl
from jax.experimental.pallas import tpu as pltpu
from jax.sharding import PartitionSpec as P

NO = 120
NV = 600
TILE = 128
WIDTH = 128
MESH = pl.DeviceIdType.MESH


def split_index(ids, size):
    quotient = ((ids.astype(jnp.float32) + 0.5) * (1.0 / size)).astype(jnp.int32)
    return quotient, ids - quotient * size


def halves(values):
    high = values.astype(jnp.bfloat16)
    return high, (values - high.astype(jnp.float32)).astype(jnp.bfloat16)


def kernel(
    n_amp, n_int,
    t2_order, int_order, blk_len, t2, own_b, driver, eps_occ, eps_vir, out,
    unit, gathered, a_high, a_low, other_b, partial, arrived, vir_sum,
    b_send, b_recv, u_send, u_recv, y_send, core_send, g_recv, r_send, r_recv,
):
    amp = lax.axis_index("amp")
    q = lax.axis_index("int")
    groups = n_amp // 2
    ys = n_int // 2
    g, h = amp // 2, amp % 2
    y, core = q // 2, q % 2
    rows = t2.shape[0]
    slots = t2.shape[1] // TILE
    owned = own_b.shape[0] // TILE
    chunks = own_b.shape[1] // WIDTH
    partner = (g * 2 + 1 - h, q)
    sibling = (amp, y * 2 + 1 - core)

    def member(group):
        return (group * 2 + h, q)

    peers = [partner, sibling]
    peers += [member((g + k) % groups) for k in range(1, groups)]
    peers += [(amp, (y + k) % ys * 2 + core) for k in range(1, ys)]
    barrier = pltpu.get_barrier_semaphore()
    for peer in peers:
        pl.semaphore_signal(barrier, inc=1, device_id=peer, device_id_type=MESH)
    pl.semaphore_wait(barrier, len(peers))

    def remote(src, dst, send, recv, peer):
        return pltpu.make_async_remote_copy(
            src_ref=src, dst_ref=dst, send_sem=send, recv_sem=recv, device_id=peer, device_id_type=MESH
        )

    def b_copy(c):
        cols = pl.ds(pl.multiple_of(c * WIDTH, WIDTH), WIDTH)
        return remote(own_b.at[:, cols], other_b.at[c], b_send.at[c], b_recv.at[c], partner)

    @pl.loop(0, chunks)
    def _(c):
        b_copy(c).start()

    lane = lax.broadcasted_iota(jnp.int32, (rows, TILE), 1)

    def u_copy(group):
        return remote(unit.at[group], gathered.at[q, g], u_send.at[group], u_recv.at[g], member(group))

    def u_arrival(group):
        return remote(unit.at[group], gathered.at[q, group], u_send.at[group], u_recv.at[group], member(group))

    stored = [t2_order[q * slots + k] for k in range(slots)]
    lengths = []
    for k in range(slots):
        length = jnp.int32(0)
        for b in range(n_amp * owned):
            length += (stored[k] == b).astype(jnp.int32) * blk_len[b]
        lengths.append(length)

    def build(group):
        for side in range(2):
            p = group * 2 + (h if side == 0 else 1 - h)
            wanted = [int_order[p * owned + j] for j in range(owned)]
            total = jnp.zeros((rows, TILE), jnp.float32)
            for k in range(slots):
                held = jnp.int32(0)
                for block in wanted:
                    held += (stored[k] == block).astype(jnp.int32)
                total = jnp.where(lane < held * lengths[k], t2[:, k * TILE:(k + 1) * TILE], total)
            unit[group, :, side * TILE:(side + 1) * TILE] = total

    for k in range(1, groups):
        group = (g + k) % groups
        build(group)
        u_copy(group).start()
    build(g)
    gathered[q, g] = unit[g]

    def y_copy(k, group):
        return remote(
            gathered.at[q, group], gathered.at[q, group], y_send.at[k, group], g_recv.at[q, group],
            (amp, (y + k) % ys * 2 + core),
        )

    def core_copy(row, group):
        return remote(
            gathered.at[row, group], gathered.at[row, group], core_send.at[row, group], g_recv.at[row, group], sibling
        )

    def arrival(row, group):
        return remote(
            gathered.at[row, group], gathered.at[row, group], core_send.at[row, group], g_recv.at[row, group], sibling
        )

    for k in range(groups):
        group = (g + k) % groups
        if k > 0:
            u_arrival(group).wait_recv()
        for m in range(1, ys):
            y_copy(m, group).start()
        core_copy(q, group).start()


    row_ids = amp * rows + lax.broadcasted_iota(jnp.int32, (rows, NO), 0)
    place = lax.broadcasted_iota(jnp.int32, (rows, NO), 1)
    first, second = split_index(row_ids, NO)
    occ = jnp.broadcast_to(eps_occ[...], (rows, NO))
    occ_first = jnp.sum(jnp.where(place == first, occ, 0.0), axis=1, keepdims=True)
    occ_second = jnp.sum(jnp.where(place == second, occ, 0.0), axis=1, keepdims=True)

    @pl.loop(0, chunks)
    def _(t):
        col_ids = q * own_b.shape[1] + t * WIDTH + lax.broadcasted_iota(jnp.int32, (NV, WIDTH), 1)
        spot = lax.broadcasted_iota(jnp.int32, (NV, WIDTH), 0)
        around, first_vir = split_index(col_ids, NV)
        second_vir = split_index(3 * col_ids + around, NV)[1]
        picks = (spot == first_vir).astype(jnp.float32) + (spot == second_vir).astype(jnp.float32)
        vir_sum[t] = jnp.dot(
            jnp.broadcast_to(eps_vir[...].reshape(1, NV), (8, NV)), picks,
            precision=lax.Precision.HIGHEST, preferred_element_type=jnp.float32,
        )

    for k in range(groups):
        group = (g + k) % groups
        for m in range(1, ys):
            row = (y + m) % ys * 2 + core
            arrival(row, group).wait_recv()
            core_copy(row, group).start()
    shares = []
    for side in range(2):
        p = g * 2 + (h if side == 0 else 1 - h)
        for j in range(owned):
            block = int_order[p * owned + j]
            found = []
            for source in range(n_int):
                share = jnp.int32(0)
                for k in range(slots):
                    share += (t2_order[source * slots + k] == block).astype(jnp.int32)
                found.append(share)
            shares.append(found)
    for k in range(groups):
        group = (g + k) % groups
        for m in range(ys):
            arrival((y + m) % ys * 2 + 1 - core, group).wait_recv()
        for place_of, found in enumerate(shares):
            side = place_of // owned
            picked = jnp.zeros((rows, TILE), jnp.float32)
            for source in range(n_int):
                piece = gathered[source, group, :, side * TILE:(side + 1) * TILE]
                picked = jnp.where(jnp.full((rows, TILE), found[source], jnp.int32) > 0, piece, picked)
            high, low = halves(picked)
            spot = (pl.ds(pl.multiple_of(group * rows, rows), rows), pl.ds(place_of * TILE, TILE))
            a_high[spot] = high
            a_low[spot] = low

    def forward_copy(c, d, slot, group):
        return remote(partial.at[c, d], arrived.at[c, slot], r_send.at[c, d], r_recv.at[c, slot], member(group))

    def take_in(c, d, slot):
        remote(
            partial.at[c, d], arrived.at[c, slot], r_send.at[c, d], r_recv.at[c, slot], partner
        ).wait_recv()
        partial[c, d] += arrived[c, slot]

    @pl.loop(0, chunks + groups - 1)
    def _(t):
        @pl.when(t < chunks)
        def _():
            cols = pl.ds(pl.multiple_of(t * WIDTH, WIDTH), WIDTH)
            b_copy(t).wait_recv()
            high, low = halves(jnp.concatenate([own_b[:, cols], other_b[t]], axis=0))
            dot = functools.partial(jnp.dot, preferred_element_type=jnp.float32)
            product = dot(a_low[...], high) + dot(a_high[...], low) + dot(a_high[...], high)
            partial[t] = product.reshape(groups, rows, WIDTH)

        right = t - g
        left = t - (groups - 1 - g)

        @pl.when((right >= 0) & (right < chunks))
        def _():
            for d in range(groups - 1, 0, -1):
                @pl.when(d > g)
                def _(d=d):
                    @pl.when(g > 0)
                    def _():
                        take_in(right, d, d)
                    forward_copy(right, d, d, g + 1).start()

        @pl.when((left >= 0) & (left < chunks))
        def _():
            for d in range(groups - 1):
                @pl.when(d < g)
                def _(d=d):
                    @pl.when(g < groups - 1)
                    def _():
                        take_in(left, d, d)
                    forward_copy(left, d, jnp.where(d == g - 1, groups, d), g - 1).start()

        done = t - (groups - 1)

        @pl.when(done >= 0)
        def _():
            @pl.when(g > 0)
            def _():
                take_in(done, g, g)

            @pl.when(g < groups - 1)
            def _():
                take_in(done, g, groups)
            cols = pl.ds(pl.multiple_of(done * WIDTH, WIDTH), WIDTH)
            length = blk_len[q * chunks + done]
            live = (lane < length).astype(jnp.float32)
            denominators = vir_sum[done, 0:1, :] - occ_first - occ_second
            out[:, cols] = (driver[:, cols] + partial[done, g]) * live / denominators

    @pl.loop(0, chunks)
    def _(c):
        b_copy(c).wait_send()
        for d in range(groups):
            @pl.when(d != g)
            def _(d=d):
                forward_copy(c, d, d, g).wait_send()
    for k in range(1, groups):
        u_copy((g + k) % groups).wait_send()
    for group in range(groups):
        for m in range(1, ys):
            y_copy(m, group).wait_send()
        for m in range(ys):
            core_copy((y + m) % ys * 2 + core, group).wait_send()


def solution(mesh):
    n_amp, n_int = mesh.shape["amp"], mesh.shape["int"]

    def on_device(t2_stored, integrals, driver, eps_occ, eps_vir, blk_len, t2_order, int_order):
        rows = t2_stored.shape[0]
        depth, cols = integrals.shape
        groups, ys, chunks = n_amp // 2, n_int // 2, cols // WIDTH
        smem = pl.BlockSpec(memory_space=pltpu.SMEM)
        vmem = pl.BlockSpec(memory_space=pltpu.VMEM)
        dma = pltpu.SemaphoreType.DMA
        return pl.pallas_call(
            functools.partial(kernel, n_amp, n_int),
            out_shape=jax.ShapeDtypeStruct((rows, cols), jnp.float32),
            in_specs=[smem] * 3 + [vmem] * 5,
            out_specs=vmem,
            scratch_shapes=[
                pltpu.VMEM((groups, rows, 2 * TILE), jnp.float32),
                pltpu.VMEM((n_int, groups, rows, 2 * TILE), jnp.float32),
                pltpu.VMEM((groups * rows, n_int * 2 * TILE), jnp.bfloat16),
                pltpu.VMEM((groups * rows, n_int * 2 * TILE), jnp.bfloat16),
                pltpu.VMEM((chunks, depth, WIDTH), jnp.float32),
                pltpu.VMEM((chunks, groups, rows, WIDTH), jnp.float32),
                pltpu.VMEM((chunks, groups + 1, rows, WIDTH), jnp.float32),
                pltpu.VMEM((chunks, 8, WIDTH), jnp.float32),
                dma((chunks,)),
                dma((chunks,)),
                dma((groups,)),
                dma((groups,)),
                dma((ys, groups)),
                dma((n_int, groups)),
                dma((n_int, groups)),
                dma((chunks, groups)),
                dma((chunks, groups + 1)),
            ],
            compiler_params=pltpu.CompilerParams(
                collective_id=0, has_side_effects=True, vmem_limit_bytes=60 * 2**20
            ),
            cost_estimate=pl.CostEstimate(flops=6 * rows * groups * depth * 2 * cols, bytes_accessed=2**23, transcendentals=0),
        )(
            t2_order, int_order, blk_len, t2_stored, integrals, driver,
            eps_occ.reshape(1, NO), eps_vir,
        )

    placed = (P("amp", "int"), P("amp", "int"), P("amp", "int"), P(), P(), P(), P(), P())
    return jax.shard_map(on_device, mesh=mesh, in_specs=placed, out_specs=P("amp", "int"), check_vma=False)
```

```python
import functools

import jax
import jax.numpy as jnp
from jax import lax
from jax.experimental import pallas as pl
from jax.experimental.pallas import tpu as pltpu
from jax.sharding import PartitionSpec as P

NO = 120
NV = 600
TILE = 128
WIDTH = 256
MESH = pl.DeviceIdType.MESH


def split_index(ids, size):
    quotient = ((ids.astype(jnp.float32) + 0.5) * (1.0 / size)).astype(jnp.int32)
    return quotient, ids - quotient * size


def halves(values):
    high = values.astype(jnp.bfloat16)
    return high, (values - high.astype(jnp.float32)).astype(jnp.bfloat16)


def kernel(
    n_amp, n_int,
    t2_order, int_order, blk_len, t2, own_b, driver, eps_occ, eps_vir, out,
    unit, gathered, a_high, a_low, other_b, partial, arrived, vir_sum,
    b_send, b_recv, u_send, u_recv, y_send, core_send, g_recv, r_send, r_recv,
):
    amp = lax.axis_index("amp")
    q = lax.axis_index("int")
    groups = n_amp // 2
    ys = n_int // 2
    g, h = amp // 2, amp % 2
    y, core = q // 2, q % 2
    rows = t2.shape[0]
    slots = t2.shape[1] // TILE
    owned = own_b.shape[0] // TILE
    chunks = own_b.shape[1] // WIDTH
    partner = (g * 2 + 1 - h, q)
    sibling = (amp, y * 2 + 1 - core)

    def member(group):
        return (group * 2 + h, q)

    peers = [partner, sibling]
    peers += [member((g + k) % groups) for k in range(1, groups)]
    peers += [(amp, (y + k) % ys * 2 + core) for k in range(1, ys)]
    barrier = pltpu.get_barrier_semaphore()
    for peer in peers:
        pl.semaphore_signal(barrier, inc=1, device_id=peer, device_id_type=MESH)
    pl.semaphore_wait(barrier, len(peers))

    def remote(src, dst, send, recv, peer):
        return pltpu.make_async_remote_copy(
            src_ref=src, dst_ref=dst, send_sem=send, recv_sem=recv, device_id=peer, device_id_type=MESH
        )

    def b_copy(c):
        cols = pl.ds(pl.multiple_of(c * WIDTH, WIDTH), WIDTH)
        return remote(own_b.at[:, cols], other_b.at[c], b_send.at[c], b_recv.at[c], partner)

    @pl.loop(0, chunks)
    def _(c):
        b_copy(c).start()

    lane = lax.broadcasted_iota(jnp.int32, (rows, TILE), 1)

    def u_copy(group):
        return remote(unit.at[group], gathered.at[q, g], u_send.at[group], u_recv.at[g], member(group))

    def u_arrival(group):
        return remote(unit.at[group], gathered.at[q, group], u_send.at[group], u_recv.at[group], member(group))

    stored = [t2_order[q * slots + k] for k in range(slots)]
    lengths = []
    for k in range(slots):
        length = jnp.int32(0)
        for b in range(n_amp * owned):
            length += (stored[k] == b).astype(jnp.int32) * blk_len[b]
        lengths.append(length)

    def build(group):
        for side in range(2):
            p = group * 2 + (h if side == 0 else 1 - h)
            wanted = [int_order[p * owned + j] for j in range(owned)]
            total = jnp.zeros((rows, TILE), jnp.float32)
            for k in range(slots):
                held = jnp.int32(0)
                for block in wanted:
                    held += (stored[k] == block).astype(jnp.int32)
                total = jnp.where(lane < held * lengths[k], t2[:, k * TILE:(k + 1) * TILE], total)
            unit[group, :, side * TILE:(side + 1) * TILE] = total

    for k in range(1, groups):
        group = (g + k) % groups
        build(group)
        u_copy(group).start()
    build(g)
    gathered[q, g] = unit[g]

    def y_copy(k, group):
        return remote(
            gathered.at[q, group], gathered.at[q, group], y_send.at[k, group], g_recv.at[q, group],
            (amp, (y + k) % ys * 2 + core),
        )

    def core_copy(row, group):
        return remote(
            gathered.at[row, group], gathered.at[row, group], core_send.at[row, group], g_recv.at[row, group], sibling
        )

    def arrival(row, group):
        return remote(
            gathered.at[row, group], gathered.at[row, group], core_send.at[row, group], g_recv.at[row, group], sibling
        )

    for k in range(groups):
        group = (g + k) % groups
        if k > 0:
            u_arrival(group).wait_recv()
        for m in range(1, ys):
            y_copy(m, group).start()
        core_copy(q, group).start()


    row_ids = amp * rows + lax.broadcasted_iota(jnp.int32, (rows, NO), 0)
    place = lax.broadcasted_iota(jnp.int32, (rows, NO), 1)
    first, second = split_index(row_ids, NO)
    occ = jnp.broadcast_to(eps_occ[...], (rows, NO))
    occ_first = jnp.sum(jnp.where(place == first, occ, 0.0), axis=1, keepdims=True)
    occ_second = jnp.sum(jnp.where(place == second, occ, 0.0), axis=1, keepdims=True)

    @pl.loop(0, chunks)
    def _(t):
        col_ids = q * own_b.shape[1] + t * WIDTH + lax.broadcasted_iota(jnp.int32, (NV, WIDTH), 1)
        spot = lax.broadcasted_iota(jnp.int32, (NV, WIDTH), 0)
        around, first_vir = split_index(col_ids, NV)
        second_vir = split_index(3 * col_ids + around, NV)[1]
        picks = (spot == first_vir).astype(jnp.float32) + (spot == second_vir).astype(jnp.float32)
        vir_sum[t] = jnp.dot(
            jnp.broadcast_to(eps_vir[...].reshape(1, NV), (8, NV)), picks,
            precision=lax.Precision.HIGHEST, preferred_element_type=jnp.float32,
        )

    for k in range(groups):
        group = (g + k) % groups
        for m in range(1, ys):
            row = (y + m) % ys * 2 + core
            arrival(row, group).wait_recv()
            core_copy(row, group).start()
    shares = []
    for side in range(2):
        p = g * 2 + (h if side == 0 else 1 - h)
        for j in range(owned):
            block = int_order[p * owned + j]
            found = []
            for source in range(n_int):
                share = jnp.int32(0)
                for k in range(slots):
                    share += (t2_order[source * slots + k] == block).astype(jnp.int32)
                found.append(share)
            shares.append(found)
    for k in range(groups):
        group = (g + k) % groups
        for m in range(ys):
            arrival((y + m) % ys * 2 + 1 - core, group).wait_recv()
        for place_of, found in enumerate(shares):
            side = place_of // owned
            picked = jnp.zeros((rows, TILE), jnp.float32)
            for source in range(n_int):
                piece = gathered[source, group, :, side * TILE:(side + 1) * TILE]
                picked = jnp.where(jnp.full((rows, TILE), found[source], jnp.int32) > 0, piece, picked)
            high, low = halves(picked)
            spot = (pl.ds(pl.multiple_of(group * rows, rows), rows), pl.ds(place_of * TILE, TILE))
            a_high[spot] = high
            a_low[spot] = low

    def forward_copy(c, d, slot, group):
        return remote(partial.at[c, d], arrived.at[c, slot], r_send.at[c, d], r_recv.at[c, slot], member(group))

    def take_in(c, d, slot):
        remote(
            partial.at[c, d], arrived.at[c, slot], r_send.at[c, d], r_recv.at[c, slot], partner
        ).wait_recv()
        partial[c, d] += arrived[c, slot]

    @pl.loop(0, chunks + groups - 1)
    def _(t):
        @pl.when(t < chunks)
        def _():
            cols = pl.ds(pl.multiple_of(t * WIDTH, WIDTH), WIDTH)
            b_copy(t).wait_recv()
            high, low = halves(jnp.concatenate([own_b[:, cols], other_b[t]], axis=0))
            dot = functools.partial(jnp.dot, preferred_element_type=jnp.float32)
            product = dot(a_low[...], high) + dot(a_high[...], low) + dot(a_high[...], high)
            partial[t] = product.reshape(groups, rows, WIDTH)

        right = t - g
        left = t - (groups - 1 - g)

        @pl.when((right >= 0) & (right < chunks))
        def _():
            for d in range(groups - 1, 0, -1):
                @pl.when(d > g)
                def _(d=d):
                    @pl.when(g > 0)
                    def _():
                        take_in(right, d, d)
                    forward_copy(right, d, d, g + 1).start()

        @pl.when((left >= 0) & (left < chunks))
        def _():
            for d in range(groups - 1):
                @pl.when(d < g)
                def _(d=d):
                    @pl.when(g < groups - 1)
                    def _():
                        take_in(left, d, d)
                    forward_copy(left, d, jnp.where(d == g - 1, groups, d), g - 1).start()

        done = t - (groups - 1)

        @pl.when(done >= 0)
        def _():
            @pl.when(g > 0)
            def _():
                take_in(done, g, g)

            @pl.when(g < groups - 1)
            def _():
                take_in(done, g, groups)
            cols = pl.ds(pl.multiple_of(done * WIDTH, WIDTH), WIDTH)
            tiles = WIDTH // TILE
            live = jnp.concatenate(
                [(lane < blk_len[(q * chunks + done) * tiles + i]).astype(jnp.float32) for i in range(tiles)], axis=1
            )
            denominators = vir_sum[done, 0:1, :] - occ_first - occ_second
            out[:, cols] = (driver[:, cols] + partial[done, g]) * live / denominators

    @pl.loop(0, chunks)
    def _(c):
        b_copy(c).wait_send()
        for d in range(groups):
            @pl.when(d != g)
            def _(d=d):
                forward_copy(c, d, d, g).wait_send()
    for k in range(1, groups):
        u_copy((g + k) % groups).wait_send()
    for group in range(groups):
        for m in range(1, ys):
            y_copy(m, group).wait_send()
        for m in range(ys):
            core_copy((y + m) % ys * 2 + core, group).wait_send()


def solution(mesh):
    n_amp, n_int = mesh.shape["amp"], mesh.shape["int"]

    def on_device(t2_stored, integrals, driver, eps_occ, eps_vir, blk_len, t2_order, int_order):
        rows = t2_stored.shape[0]
        depth, cols = integrals.shape
        groups, ys, chunks = n_amp // 2, n_int // 2, cols // WIDTH
        smem = pl.BlockSpec(memory_space=pltpu.SMEM)
        vmem = pl.BlockSpec(memory_space=pltpu.VMEM)
        dma = pltpu.SemaphoreType.DMA
        return pl.pallas_call(
            functools.partial(kernel, n_amp, n_int),
            out_shape=jax.ShapeDtypeStruct((rows, cols), jnp.float32),
            in_specs=[smem] * 3 + [vmem] * 5,
            out_specs=vmem,
            scratch_shapes=[
                pltpu.VMEM((groups, rows, 2 * TILE), jnp.float32),
                pltpu.VMEM((n_int, groups, rows, 2 * TILE), jnp.float32),
                pltpu.VMEM((groups * rows, n_int * 2 * TILE), jnp.bfloat16),
                pltpu.VMEM((groups * rows, n_int * 2 * TILE), jnp.bfloat16),
                pltpu.VMEM((chunks, depth, WIDTH), jnp.float32),
                pltpu.VMEM((chunks, groups, rows, WIDTH), jnp.float32),
                pltpu.VMEM((chunks, groups + 1, rows, WIDTH), jnp.float32),
                pltpu.VMEM((chunks, 8, WIDTH), jnp.float32),
                dma((chunks,)),
                dma((chunks,)),
                dma((groups,)),
                dma((groups,)),
                dma((ys, groups)),
                dma((n_int, groups)),
                dma((n_int, groups)),
                dma((chunks, groups)),
                dma((chunks, groups + 1)),
            ],
            compiler_params=pltpu.CompilerParams(
                collective_id=0, has_side_effects=True, vmem_limit_bytes=60 * 2**20
            ),
            cost_estimate=pl.CostEstimate(flops=6 * rows * groups * depth * 2 * cols, bytes_accessed=2**23, transcendentals=0),
        )(
            t2_order, int_order, blk_len, t2_stored, integrals, driver,
            eps_occ.reshape(1, NO), eps_vir,
        )

    placed = (P("amp", "int"), P("amp", "int"), P("amp", "int"), P(), P(), P(), P(), P())
    return jax.shard_map(on_device, mesh=mesh, in_specs=placed, out_specs=P("amp", "int"), check_vma=False)
```

```python
import functools

import jax
import jax.numpy as jnp
from jax import lax
from jax.experimental import pallas as pl
from jax.experimental.pallas import tpu as pltpu
from jax.sharding import PartitionSpec as P

NO = 120
NV = 600
TILE = 128
WIDTH = 256
MESH = pl.DeviceIdType.MESH


def split_index(ids, size):
    quotient = ((ids.astype(jnp.float32) + 0.5) * (1.0 / size)).astype(jnp.int32)
    return quotient, ids - quotient * size


def halves(values):
    high = values.astype(jnp.bfloat16)
    return high, (values - high.astype(jnp.float32)).astype(jnp.bfloat16)


def kernel(
    n_amp, n_int,
    t2_order, int_order, blk_len, t2, own_b, driver, eps_occ, eps_vir, out,
    unit, gathered, a_high, a_low, other_b, partial, arrived, vir_sum,
    b_send, b_recv, u_send, u_recv, y_send, core_send, g_recv, r_send, r_recv,
):
    amp = lax.axis_index("amp")
    q = lax.axis_index("int")
    groups = n_amp // 2
    ys = n_int // 2
    g, h = amp // 2, amp % 2
    y, core = q // 2, q % 2
    rows = t2.shape[0]
    slots = t2.shape[1] // TILE
    owned = own_b.shape[0] // TILE
    chunks = own_b.shape[1] // WIDTH
    partner = (g * 2 + 1 - h, q)
    sibling = (amp, y * 2 + 1 - core)

    def member(group):
        return (group * 2 + h, q)

    peers = [partner, sibling]
    peers += [member((g + k) % groups) for k in range(1, groups)]
    peers += [(amp, (y + k) % ys * 2 + core) for k in range(1, ys)]
    barrier = pltpu.get_barrier_semaphore()
    for peer in peers:
        pl.semaphore_signal(barrier, inc=1, device_id=peer, device_id_type=MESH)
    pl.semaphore_wait(barrier, len(peers))

    def remote(src, dst, send, recv, peer):
        return pltpu.make_async_remote_copy(
            src_ref=src, dst_ref=dst, send_sem=send, recv_sem=recv, device_id=peer, device_id_type=MESH
        )

    def b_copy(c):
        cols = pl.ds(pl.multiple_of(c * WIDTH, WIDTH), WIDTH)
        return remote(own_b.at[:, cols], other_b.at[c], b_send.at[c], b_recv.at[c], partner)

    @pl.loop(0, chunks)
    def _(c):
        b_copy(c).start()

    lane = lax.broadcasted_iota(jnp.int32, (rows, TILE), 1)

    def u_copy(group):
        return remote(unit.at[group], gathered.at[q, g], u_send.at[group], u_recv.at[g], member(group))

    def u_arrival(group):
        return remote(unit.at[group], gathered.at[q, group], u_send.at[group], u_recv.at[group], member(group))

    stored = [t2_order[q * slots + k] for k in range(slots)]
    lengths = []
    for k in range(slots):
        length = jnp.int32(0)
        for b in range(n_amp * owned):
            length += (stored[k] == b).astype(jnp.int32) * blk_len[b]
        lengths.append(length)

    def build(group):
        for side in range(2):
            p = group * 2 + (h if side == 0 else 1 - h)
            wanted = [int_order[p * owned + j] for j in range(owned)]
            total = jnp.zeros((rows, TILE), jnp.float32)
            for k in range(slots):
                held = jnp.int32(0)
                for block in wanted:
                    held += (stored[k] == block).astype(jnp.int32)
                total = jnp.where(lane < held * lengths[k], t2[:, k * TILE:(k + 1) * TILE], total)
            unit[group, :, side * TILE:(side + 1) * TILE] = total

    for k in range(1, groups):
        group = (g + k) % groups
        build(group)
        u_copy(group).start()
    build(g)
    gathered[q, g] = unit[g]

    def y_copy(k, group):
        return remote(
            gathered.at[q, group], gathered.at[q, group], y_send.at[k, group], g_recv.at[q, group],
            (amp, (y + k) % ys * 2 + core),
        )

    def core_copy(row, group):
        return remote(
            gathered.at[row, group], gathered.at[row, group], core_send.at[row, group], g_recv.at[row, group], sibling
        )

    def arrival(row, group):
        return remote(
            gathered.at[row, group], gathered.at[row, group], core_send.at[row, group], g_recv.at[row, group], sibling
        )

    for k in range(groups):
        group = (g + k) % groups
        if k > 0:
            u_arrival(group).wait_recv()
        for m in range(1, ys):
            y_copy(m, group).start()
        core_copy(q, group).start()


    row_ids = amp * rows + lax.broadcasted_iota(jnp.int32, (rows, NO), 0)
    place = lax.broadcasted_iota(jnp.int32, (rows, NO), 1)
    first, second = split_index(row_ids, NO)
    occ = jnp.broadcast_to(eps_occ[...], (rows, NO))
    occ_first = jnp.sum(jnp.where(place == first, occ, 0.0), axis=1, keepdims=True)
    occ_second = jnp.sum(jnp.where(place == second, occ, 0.0), axis=1, keepdims=True)

    @pl.loop(0, chunks)
    def _(t):
        col_ids = q * own_b.shape[1] + t * WIDTH + lax.broadcasted_iota(jnp.int32, (NV, WIDTH), 1)
        spot = lax.broadcasted_iota(jnp.int32, (NV, WIDTH), 0)
        around, first_vir = split_index(col_ids, NV)
        second_vir = split_index(3 * col_ids + around, NV)[1]
        picks = (spot == first_vir).astype(jnp.float32) + (spot == second_vir).astype(jnp.float32)
        vir_sum[t] = jnp.dot(
            jnp.broadcast_to(eps_vir[...].reshape(1, NV), (8, NV)), picks,
            precision=lax.Precision.HIGHEST, preferred_element_type=jnp.float32,
        )

    for k in range(groups):
        group = (g + k) % groups
        for m in range(1, ys):
            row = (y + m) % ys * 2 + core
            arrival(row, group).wait_recv()
            core_copy(row, group).start()
    shares = []
    for side in range(2):
        p = g * 2 + (h if side == 0 else 1 - h)
        for j in range(owned):
            block = int_order[p * owned + j]
            found = []
            for source in range(n_int):
                share = jnp.int32(0)
                for k in range(slots):
                    share += (t2_order[source * slots + k] == block).astype(jnp.int32)
                found.append(share)
            shares.append(found)
    for k in range(groups):
        group = (g + k) % groups
        for m in range(ys):
            arrival((y + m) % ys * 2 + 1 - core, group).wait_recv()
        for place_of, found in enumerate(shares):
            side = place_of // owned
            picked = jnp.zeros((rows, TILE), jnp.float32)
            for source in range(n_int):
                piece = gathered[source, group, :, side * TILE:(side + 1) * TILE]
                picked = jnp.where(jnp.full((rows, TILE), found[source], jnp.int32) > 0, piece, picked)
            high, low = halves(picked)
            spot = (pl.ds(pl.multiple_of(group * rows, rows), rows), pl.ds(place_of * TILE, TILE))
            a_high[spot] = high
            a_low[spot] = low

    def forward_copy(c, d, slot, group):
        return remote(partial.at[c, d], arrived.at[c, slot], r_send.at[c, d], r_recv.at[c, slot], member(group))

    def take_in(c, d, slot):
        remote(
            partial.at[c, d], arrived.at[c, slot], r_send.at[c, d], r_recv.at[c, slot], partner
        ).wait_recv()
        partial[c, d] += arrived[c, slot]

    @pl.loop(0, chunks + groups - 1)
    def _(t):
        right = t - g
        left = t - (groups - 1 - g)

        @pl.when((g > 0) & (right >= 0) & (right < chunks))
        def _():
            for d in range(groups - 1, 0, -1):
                @pl.when(d > g)
                def _(d=d):
                    take_in(right, d, d)
                    forward_copy(right, d, d, g + 1).start()

        @pl.when((g < groups - 1) & (left >= 0) & (left < chunks))
        def _():
            for d in range(groups - 1):
                @pl.when(d < g)
                def _(d=d):
                    take_in(left, d, d)
                    forward_copy(left, d, jnp.where(d == g - 1, groups, d), g - 1).start()

        @pl.when(t < chunks)
        def _():
            cols = pl.ds(pl.multiple_of(t * WIDTH, WIDTH), WIDTH)
            b_copy(t).wait_recv()
            high, low = halves(jnp.concatenate([own_b[:, cols], other_b[t]], axis=0))
            dot = functools.partial(jnp.dot, preferred_element_type=jnp.float32)
            product = dot(a_low[...], high) + dot(a_high[...], low) + dot(a_high[...], high)
            partial[t] = product.reshape(groups, rows, WIDTH)

        @pl.when((g == 0) & (t < chunks))
        def _():
            for d in range(groups - 1, 0, -1):
                forward_copy(t, d, d, 1).start()

        @pl.when((g == groups - 1) & (t < chunks))
        def _():
            for d in range(groups - 1):
                forward_copy(t, d, groups if d == groups - 2 else d, groups - 2).start()

        done = t - (groups - 1)

        @pl.when(done >= 0)
        def _():
            @pl.when(g > 0)
            def _():
                take_in(done, g, g)

            @pl.when(g < groups - 1)
            def _():
                take_in(done, g, groups)
            cols = pl.ds(pl.multiple_of(done * WIDTH, WIDTH), WIDTH)
            tiles = WIDTH // TILE
            live = jnp.concatenate(
                [(lane < blk_len[(q * chunks + done) * tiles + i]).astype(jnp.float32) for i in range(tiles)], axis=1
            )
            denominators = vir_sum[done, 0:1, :] - occ_first - occ_second
            out[:, cols] = (driver[:, cols] + partial[done, g]) * live / denominators

    @pl.loop(0, chunks)
    def _(c):
        b_copy(c).wait_send()
        for d in range(groups):
            @pl.when(d != g)
            def _(d=d):
                forward_copy(c, d, d, g).wait_send()
    for k in range(1, groups):
        u_copy((g + k) % groups).wait_send()
    for group in range(groups):
        for m in range(1, ys):
            y_copy(m, group).wait_send()
        for m in range(ys):
            core_copy((y + m) % ys * 2 + core, group).wait_send()


def solution(mesh):
    n_amp, n_int = mesh.shape["amp"], mesh.shape["int"]

    def on_device(t2_stored, integrals, driver, eps_occ, eps_vir, blk_len, t2_order, int_order):
        rows = t2_stored.shape[0]
        depth, cols = integrals.shape
        groups, ys, chunks = n_amp // 2, n_int // 2, cols // WIDTH
        smem = pl.BlockSpec(memory_space=pltpu.SMEM)
        vmem = pl.BlockSpec(memory_space=pltpu.VMEM)
        dma = pltpu.SemaphoreType.DMA
        return pl.pallas_call(
            functools.partial(kernel, n_amp, n_int),
            out_shape=jax.ShapeDtypeStruct((rows, cols), jnp.float32),
            in_specs=[smem] * 3 + [vmem] * 5,
            out_specs=vmem,
            scratch_shapes=[
                pltpu.VMEM((groups, rows, 2 * TILE), jnp.float32),
                pltpu.VMEM((n_int, groups, rows, 2 * TILE), jnp.float32),
                pltpu.VMEM((groups * rows, n_int * 2 * TILE), jnp.bfloat16),
                pltpu.VMEM((groups * rows, n_int * 2 * TILE), jnp.bfloat16),
                pltpu.VMEM((chunks, depth, WIDTH), jnp.float32),
                pltpu.VMEM((chunks, groups, rows, WIDTH), jnp.float32),
                pltpu.VMEM((chunks, groups + 1, rows, WIDTH), jnp.float32),
                pltpu.VMEM((chunks, 8, WIDTH), jnp.float32),
                dma((chunks,)),
                dma((chunks,)),
                dma((groups,)),
                dma((groups,)),
                dma((ys, groups)),
                dma((n_int, groups)),
                dma((n_int, groups)),
                dma((chunks, groups)),
                dma((chunks, groups + 1)),
            ],
            compiler_params=pltpu.CompilerParams(
                collective_id=0, has_side_effects=True, vmem_limit_bytes=60 * 2**20
            ),
            cost_estimate=pl.CostEstimate(flops=6 * rows * groups * depth * 2 * cols, bytes_accessed=2**23, transcendentals=0),
        )(
            t2_order, int_order, blk_len, t2_stored, integrals, driver,
            eps_occ.reshape(1, NO), eps_vir,
        )

    placed = (P("amp", "int"), P("amp", "int"), P("amp", "int"), P(), P(), P(), P(), P())
    return jax.shard_map(on_device, mesh=mesh, in_specs=placed, out_specs=P("amp", "int"), check_vma=False)
```
